128 devices in a mesh: grp: 8 (over x, core), grid: 16 (over z, y).
Axes of the slice: x: 4, y: 4, z: 4, core: 2. Of those that a mesh axis runs over, the one named last changes fastest.
Arguments:
- dy_quant: bfloat16 [8, 8, 256, 8192], P(None, 'grp', 'grid'), may hold values from -4 to 4
- dy_scale: bfloat16 [8, 8, 256, 64], P(None, 'grp', 'grid'), may hold values from 0.049804688 to 1
- tokens: bfloat16 [8, 8, 256, 5120], P(None, 'grp', 'grid'), may hold values from -1.1953125 to 1.1953125
- weight: bfloat16 [8, 16, 1280, 2048], P('grp', 'grid'), may hold values from -0.078125 to 0.078125
- counts: int32 [8, 8], replicated, may hold values from 1 to 256, as said below
Outputs:
- dx_quant: bfloat16 [8, 8, 256, 5120], P(None, 'grp', 'grid')
- dx_scale: bfloat16 [8, 8, 256, 40], P(None, 'grp', 'grid')
- dw_quant: bfloat16 [8, 16, 1280, 2048], P('grp', 'grid')
- dw_scale: float32 [8, 16, 10, 16], P('grp', 'grid')
The draws below stay inside these ranges and needn't reach their ends.
Inputs may be any that keep to these rules, and one draw needn't show every extreme that they name: `counts`: some replica fills all 256 slots of some expert; the other slots of a row are padding.
All inputs are finite; a program needn't handle non-finite values. Where the reference program divides by a largest or mean magnitude, that divisor is 1e-20 or more.
Results may differ from the reference program's by a relative error of at most 0.0051.
Values may be sent and summed in bfloat16 or wider, within the bound.
A program may use at most 192 MiB of HBM per device.

```python
import math
import jax
import jax.numpy as jnp

D = 5120
FF = 8192
QB = 128
GC = 4
GR = 4
TILES = 16
CR = 256
EXPERTS = 8
N_GRP = 8


def draw_counts(key, part):
    key = jax.random.fold_in(key, 11)
    first, second, third, fourth = jax.random.split(key, 4)
    tops = jax.random.randint(first, (EXPERTS,), CR // 2, CR + 1)
    chosen = jax.random.randint(second, (), 0, EXPERTS)
    expert_ids = jnp.arange(EXPERTS, dtype=jnp.int32)
    tops = jnp.where(expert_ids == chosen, CR, tops)
    values = jax.random.randint(third, (N_GRP, EXPERTS), jnp.maximum(tops // 2, 1)[None, :], tops[None, :] + 1)
    replica = jax.random.randint(fourth, (), 0, N_GRP)
    replica_ids = jnp.arange(N_GRP, dtype=jnp.int32)
    fixed = (replica_ids[:, None] == replica) & (expert_ids[None, :] == chosen)
    return jnp.where(fixed, CR, values).astype(jnp.int32)


def shard_levels(key, shape, cuts, low, top_value):
    gain, own = 1.0, jax.random.fold_in(key, 6)
    for axis_at, shards_of in cuts:
        draws = jnp.exp(jax.random.uniform(jax.random.fold_in(own, axis_at), (shards_of,), jnp.float32, low / len(cuts), top_value / len(cuts)))
        gain = gain * jnp.repeat(draws, shape[axis_at] // shards_of).reshape([-1 if axis == axis_at else 1 for axis in range(len(shape))])
    return gain


def gaussian(stream_key, shape, scale, most, cuts=(), kind=jnp.bfloat16):
    gain = shard_levels(stream_key, shape, cuts, -0.22, 0.18) if cuts else 1.0
    array = jax.random.normal(stream_key, shape, jnp.float32) * scale * gain
    return jnp.minimum(jnp.maximum(array, -most), most).astype(kind)


def setup_inputs(seed: int = 0) -> dict:
    keys = jax.random.split(jax.random.key(seed), 6)
    return {
        "dy_quant": gaussian(keys[0], (EXPERTS, N_GRP, CR, FF), 1.0, 4.0, ((1, 8), (2, 16))),
        "dy_scale": jnp.clip(jnp.exp(math.log(1.0) - 2.9996462 * jax.random.uniform(keys[1], (EXPERTS, N_GRP, CR, FF // QB), jnp.float32) ** shard_levels(keys[1], (EXPERTS, N_GRP, CR, FF // QB), ((1, 8), (2, 16)), -0.2, 0.2)), 0.049804688, 1.0).astype(jnp.bfloat16),
        "tokens": gaussian(keys[2], (EXPERTS, N_GRP, CR, D), 0.2, 1.1953125, ((1, 8), (2, 16))),
        "weight": gaussian(keys[3], (EXPERTS, TILES, D // GR, FF // GC), D ** -0.5, 0.078125, ((0, 8), (1, 16))),
        "counts": draw_counts(jax.random.fold_in(keys[5], 71), 0),
    }


EPS = 1e-6


def to_tiles(full, rows_grid, cols_grid):
    height, width = full.shape
    blocks = full.reshape(rows_grid, height // rows_grid, cols_grid, width // cols_grid)
    return blocks.transpose(0, 2, 1, 3).reshape(rows_grid * cols_grid, height // rows_grid, width // cols_grid)


def reference(dy_quant, dy_scale, tokens, weight, counts):
    total_groups = D // QB
    col_blocks = FF // QB
    slot_ids = jnp.arange(CR, dtype=jnp.int32)
    list_xq = []
    list_xs = []
    list_wq = []
    list_ws = []
    for expert in range(EXPERTS):
        live = slot_ids[None, :] < counts[:, expert][:, None]
        values = dy_quant[expert].astype(jnp.float32).reshape(N_GRP, CR, col_blocks, QB)
        values = values * dy_scale[expert].astype(jnp.float32)[..., None]
        gradient = jnp.where(live[:, :, None], values.reshape(N_GRP, CR, FF), 0.0).astype(jnp.bfloat16)
        rows = gradient.reshape(N_GRP * CR, FF)
        full_weight = weight[expert].reshape(GR, GC, D // GR, FF // GC).transpose(0, 2, 1, 3).reshape(D, FF)
        grad_input = jnp.dot(rows, full_weight.T, preferred_element_type=jnp.float32)
        grad_weight = jnp.dot(tokens[expert].reshape(N_GRP * CR, D).T, rows, preferred_element_type=jnp.float32)
        blocks_x = grad_input.reshape(N_GRP * CR, total_groups, QB)
        scale_x = jnp.max(jnp.abs(blocks_x), axis=2) + EPS
        list_xq.append((blocks_x / scale_x[:, :, None]).reshape(N_GRP, CR, D).astype(jnp.bfloat16))
        list_xs.append(scale_x.reshape(N_GRP, CR, total_groups).astype(jnp.bfloat16))
        blocks_w = grad_weight.reshape(total_groups, QB, col_blocks, QB)
        scale_w = jnp.max(jnp.abs(blocks_w), axis=(1, 3)) + EPS
        quant_w = (blocks_w / scale_w[:, None, :, None]).reshape(D, FF).astype(jnp.bfloat16)
        list_wq.append(to_tiles(quant_w, GR, GC))
        list_ws.append(to_tiles(scale_w, GR, GC))
    return jnp.stack(list_xq), jnp.stack(list_xs), jnp.stack(list_wq), jnp.stack(list_ws)
```

```python
import functools

import jax
import jax.numpy as jnp
from jax import lax
from jax.experimental import pallas as pl
from jax.experimental.pallas import tpu as pltpu
from jax.sharding import PartitionSpec as P

QB = 128
EPS = 1e-06
SIDE = 4
ORDER = (0, 1, 3, 2)
MESH = pl.DeviceIdType.MESH
F32 = jnp.float32
BF16 = jnp.bfloat16


def kernel(
    sizes,
    counts,
    scale,
    dy,
    tokens,
    weight,
    back,
    dw_out,
    dw_scale,
    dy_in,
    grad,
    w_in,
    w_t,
    g_all,
    t_all,
    rs_send,
    rs_recv,
    own_sum,
    back_send,
    dw_sum,
    dw_quant,
    load_sem,
    g_send,
    g_recv,
    t_send,
    t_recv,
    z_send,
    z_recv,
    y_send,
    y_recv,
    r_send,
    r_recv,
    b_send,
    b_recv,
    out_sem,
):
    n_grp, shard, height, breadth = sizes
    nx = n_grp // 2
    chunk = n_grp * shard
    block = SIDE * chunk
    g = lax.axis_index("grp")
    t = lax.axis_index("grid")
    x = g // 2
    c = g % 2
    z = t // SIDE
    y = t % SIDE

    def grp_at(dx, dc):
        return ((x + dx) % nx) * 2 + (c + dc) % 2

    def z_at(d):
        return (z + d) % SIDE

    def y_at(d):
        return (y + d) % SIDE

    x_order = []
    for near in range(1, nx // 2 + 1):
        for dc in range(2):
            x_order.append((near, dc))
            if nx - near != near:
                x_order.append((nx - near, dc))
    x_order += [(0, 1), (0, 0)]

    load_dy = pltpu.make_async_copy(dy, dy_in, load_sem.at[0])
    load_w = pltpu.make_async_copy(weight, w_in, load_sem.at[1])
    load_dy.start()
    load_w.start()

    barrier = pltpu.get_barrier_semaphore()
    partners = 0
    for dx, dc in x_order:
        for d in range(SIDE):
            if (dx, dc, d) != (0, 0, 0):
                pl.semaphore_signal(
                    barrier, inc=1, device_id=(grp_at(dx, dc), z * SIDE + y_at(d)), device_id_type=MESH
                )
                partners += 1
            if d != 0:
                pl.semaphore_signal(
                    barrier, inc=1, device_id=(grp_at(dx, dc), z_at(d) * SIDE + y), device_id_type=MESH
                )
                partners += 1

    load_dy.wait()
    groups = dy_in.shape[1] // QB

    def dequantize(e, carry):
        rows = pl.ds(pl.multiple_of(e * shard, shard), shard)
        live = t * shard + lax.broadcasted_iota(jnp.int32, (shard, groups), 0) < counts[g, e]
        s = jnp.where(live, scale[rows, :].astype(F32), 0.0)
        for j in range(groups):
            cols = slice(j * QB, (j + 1) * QB)
            grad[rows, cols] = (dy_in[rows, cols].astype(F32) * s[:, j : j + 1]).astype(BF16)
        return carry

    lax.fori_loop(0, n_grp, dequantize, 0)
    pl.semaphore_wait(barrier, partners)

    mine = pl.ds(pl.multiple_of(t * chunk + g * shard, shard), shard)
    waits = []

    def remote(src, dst, send, recv, device):
        copy = pltpu.make_async_remote_copy(
            src_ref=src, dst_ref=dst, send_sem=send, recv_sem=recv, device_id=device, device_id_type=MESH
        )
        copy.start()
        waits.append(copy)

    def send_grad(d, index):
        b = y_at(d)
        cols = pl.ds(pl.multiple_of(b * breadth, breadth), breadth)
        for i, (dx, dc) in enumerate(x_order):
            e = grp_at(dx, dc)
            src = grad.at[pl.ds(pl.multiple_of(e * shard, shard), shard), cols]
            if (dx, dc, d) == (0, 0, 0):
                pltpu.make_async_copy(src, g_all.at[mine, :], g_recv.at[y]).start()
            else:
                remote(
                    src, g_all.at[mine, :], g_send.at[index * n_grp + i], g_recv.at[y], (e, z * SIDE + b)
                )

    def send_tokens(d, index):
        a = z_at(d)
        cols = pl.ds(pl.multiple_of(a * height, height), height)
        for i, (dx, dc) in enumerate(x_order):
            e = grp_at(dx, dc)
            src = tokens.at[pl.ds(pl.multiple_of(e * shard, shard), shard), cols]
            if (dx, dc, d) == (0, 0, 0):
                pltpu.make_async_copy(src, t_all.at[mine, :], t_recv.at[z]).start()
            else:
                remote(
                    src, t_all.at[mine, :], t_send.at[index * n_grp + i], t_recv.at[z], (e, a * SIDE + y)
                )

    send_grad(0, 0)
    send_grad(1, 1)
    send_tokens(0, 0)
    send_grad(3, 2)
    send_tokens(1, 1)
    send_grad(2, 3)
    send_tokens(3, 2)
    send_tokens(2, 3)

    load_w.wait()
    step = 256

    def turn(i, carry):
        rows = pl.ds(pl.multiple_of(i * step, step), step)
        for j in range(height // step):
            w_t[rows, j * step : (j + 1) * step] = w_in[j * step : (j + 1) * step, rows].T
        return carry

    lax.fori_loop(0, breadth // step, turn, 0)

    def rows_of(zs, ys):
        return pl.ds(pl.multiple_of((zs * SIDE + ys) * chunk, chunk), chunk)

    def landed(ref, sem):
        pltpu.make_async_copy(ref, ref, sem).wait()

    def input_gradient(kz, k):
        rows = rows_of(z_at(ORDER[kz]), y_at(ORDER[k]))
        slot = kz * 3 + k - 1

        def part(n, carry):
            cols = pl.ds(pl.multiple_of(n * step, step), step)
            p = jnp.dot(g_all[rows, :], w_t[:, cols], preferred_element_type=F32)
            if k == 0:
                own_sum[kz, :, cols] = p
            else:
                rs_send[slot, :, cols] = p.astype(BF16)
            return carry

        lax.fori_loop(0, height // step, part, 0)
        if k != 0:
            remote(
                rs_send.at[slot],
                rs_recv.at[slot],
                r_send.at[slot],
                r_recv.at[slot],
                (g, z * SIDE + y_at(ORDER[k])),
            )

    def reduce(kz):
        for k in range(1, SIDE):
            slot = kz * 3 + k - 1
            landed(rs_recv.at[slot], r_recv.at[slot])
        half = 16

        def part(i, carry):
            rows = pl.ds(pl.multiple_of(i * half, half), half)
            lanes = lax.broadcasted_iota(jnp.int32, (half, QB), 1)
            scales = jnp.zeros((half, QB), F32)
            for j in range(height // QB):
                cols = slice(j * QB, (j + 1) * QB)
                total = own_sum[kz, rows, cols]
                for k in range(1, SIDE):
                    total = total + rs_recv[kz * 3 + k - 1, rows, cols].astype(F32)
                s = jnp.max(jnp.abs(total), axis=1, keepdims=True) + EPS
                back_send[kz, rows, cols] = (total * (1.0 / s)).astype(BF16)
                scales = jnp.where(lanes == j, s, scales)
            back_send[kz, rows, height:] = scales.astype(BF16)
            return carry

        lax.fori_loop(0, chunk // half, part, 0)
        zs = z_at(ORDER[kz])
        dst = back.at[pl.ds(pl.multiple_of((g * SIDE + z) * shard, shard), shard), :]
        for i, (dx, dc) in enumerate(x_order):
            r = grp_at(dx, dc)
            src = back_send.at[kz, pl.ds(pl.multiple_of(r * shard, shard), shard), :]
            if (dx, dc, kz) == (0, 0, 0):
                pltpu.make_async_copy(src, dst, b_recv).start()
            else:
                remote(src, dst, b_send.at[kz * n_grp + i], b_recv, (r, zs * SIDE + y))

    wide = 512

    def weight_gradient(kz, first, last):
        rows = pl.ds(pl.multiple_of(z_at(ORDER[kz]) * block, block), block)

        def row_step(i, carry):
            down = pl.ds(pl.multiple_of(i * step, step), step)

            def col_step(j, carry):
                along = pl.ds(pl.multiple_of(j * wide, wide), wide)
                p = lax.dot_general(
                    t_all[rows, down],
                    g_all[rows, along],
                    (((0,), (0,)), ((), ())),
                    preferred_element_type=F32,
                )
                if not first:
                    p = p + dw_sum[down, along]
                if not last:
                    dw_sum[down, along] = p
                    return carry
                at_row = lax.broadcasted_iota(jnp.int32, dw_scale.shape, 0)
                at_col = lax.broadcasted_iota(jnp.int32, dw_scale.shape, 1)
                scales = dw_scale[...]
                parts = []
                for u in range(step // QB):
                    line = []
                    for v in range(wide // QB):
                        q = p[u * QB : (u + 1) * QB, v * QB : (v + 1) * QB]
                        s = jnp.max(jnp.max(jnp.abs(q), axis=0, keepdims=True), axis=1, keepdims=True) + EPS
                        line.append((q * (1.0 / s)).astype(BF16))
                        here = (at_row == i * (step // QB) + u) & (at_col == j * (wide // QB) + v)
                        scales = jnp.where(here, s, scales)
                    parts.append(jnp.concatenate(line, axis=1))
                dw_scale[...] = scales
                dw_quant[down, along] = jnp.concatenate(parts, axis=0)
                return carry

            lax.fori_loop(0, breadth // wide, col_step, 0)
            if last:
                pltpu.make_async_copy(dw_quant.at[down, :], dw_out.at[down, :], out_sem.at[i]).start()
            return carry

        lax.fori_loop(0, height // step, row_step, 0)

    def pass_grad(rows, up, sem):
        remote(
            g_all.at[rows, :],
            g_all.at[rows, :],
            z_send.at[sem],
            z_recv.at[sem],
            (g, z_at(1 if up else 3) * SIDE + y),
        )

    def pass_tokens(rows, up, sem):
        remote(
            t_all.at[rows, :],
            t_all.at[rows, :],
            y_send.at[sem],
            y_recv.at[sem],
            (g, z * SIDE + y_at(1 if up else 3)),
        )

    for k in range(SIDE):
        rows = rows_of(z, y_at(ORDER[k]))
        landed(g_all.at[rows, :], g_recv.at[y_at(ORDER[k])])
        pass_grad(rows, True, k)
        pass_grad(rows, False, 4 + k)
        rows = rows_of(z_at(ORDER[k]), y)
        landed(t_all.at[rows, :], t_recv.at[z_at(ORDER[k])])
        pass_tokens(rows, True, k)
        pass_tokens(rows, False, 4 + k)
        input_gradient(0, k)

    for k in range(SIDE):
        for up in (True, False):
            rows = rows_of(z_at(3 if up else 1), y_at(ORDER[k]))
            landed(g_all.at[rows, :], z_recv.at[k if up else 4 + k])
            if up == (k % 2 == 0):
                pass_grad(rows, up, 8 + k)
            rows = rows_of(z_at(ORDER[k]), y_at(3 if up else 1))
            landed(t_all.at[rows, :], y_recv.at[k if up else 4 + k])
            if up == (k % 2 == 0):
                pass_tokens(rows, up, 8 + k)
        input_gradient(2, k)
        input_gradient(1, k)

    reduce(0)

    for k in range(SIDE):
        landed(g_all.at[rows_of(z_at(2), y_at(ORDER[k])), :], z_recv.at[8 + k])
        input_gradient(3, k)

    reduce(1)
    reduce(2)
    for k in range(SIDE):
        landed(t_all.at[rows_of(z_at(ORDER[k]), y_at(2)), :], y_recv.at[8 + k])
    weight_gradient(0, True, False)
    weight_gradient(1, False, False)
    reduce(3)
    weight_gradient(2, False, False)
    dw_scale[...] = jnp.zeros(dw_scale.shape, F32)
    weight_gradient(3, False, True)

    for i in range(height // step):
        down = pl.ds(i * step, step)
        pltpu.make_async_copy(dw_quant.at[down, :], dw_out.at[down, :], out_sem.at[i]).wait()
    for copy in waits:
        copy.wait_send()
    landed(back, b_recv)


def on_device(dy_quant, dy_scale, tokens, weight, counts):
    n_grp, _, shard, hidden = dy_quant.shape
    width = tokens.shape[-1]
    height, breadth = weight.shape[-2:]
    rows = n_grp * shard
    slots = SIDE * SIDE * rows
    dma = pltpu.SemaphoreType.DMA
    back, dw_quant, dw_scale = pl.pallas_call(
        functools.partial(kernel, (n_grp, shard, height, breadth)),
        out_shape=(
            jax.ShapeDtypeStruct((n_grp * SIDE * shard, height + QB), BF16),
            jax.ShapeDtypeStruct((height, breadth), BF16),
            jax.ShapeDtypeStruct((height // QB, breadth // QB), F32),
        ),
        in_specs=[
            pl.BlockSpec(memory_space=pltpu.SMEM),
            pl.BlockSpec(memory_space=pltpu.VMEM),
            pl.BlockSpec(memory_space=pl.ANY),
            pl.BlockSpec(memory_space=pl.ANY),
            pl.BlockSpec(memory_space=pl.ANY),
        ],
        out_specs=(
            pl.BlockSpec(memory_space=pl.ANY),
            pl.BlockSpec(memory_space=pl.ANY),
            pl.BlockSpec(memory_space=pltpu.VMEM),
        ),
        scratch_shapes=[
            pltpu.VMEM((rows, hidden), BF16),
            pltpu.VMEM((rows, hidden), BF16),
            pltpu.VMEM((height, breadth), BF16),
            pltpu.VMEM((breadth, height), BF16),
            pltpu.VMEM((slots, breadth), BF16),
            pltpu.VMEM((slots, height), BF16),
            pltpu.VMEM((12, rows, height), BF16),
            pltpu.VMEM((12, rows, height), BF16),
            pltpu.VMEM((SIDE, rows, height), F32),
            pltpu.VMEM((SIDE, rows, height + QB), BF16),
            pltpu.VMEM((height, breadth), F32),
            pltpu.VMEM((height, breadth), BF16),
            dma((2,)),
            dma((SIDE * n_grp,)),
            dma((SIDE,)),
            dma((SIDE * n_grp,)),
            dma((SIDE,)),
            dma((12,)),
            dma((12,)),
            dma((12,)),
            dma((12,)),
            dma((12,)),
            dma((12,)),
            dma((SIDE * n_grp,)),
            dma,
            dma((height // 256,)),
        ],
        compiler_params=pltpu.CompilerParams(
            collective_id=0, has_side_effects=True, vmem_limit_bytes=62 * 2**20
        ),
        name="up_backward",
    )(
        counts,
        dy_scale.reshape(rows, hidden // QB),
        dy_quant.reshape(rows, hidden),
        tokens.reshape(rows, width),
        weight.reshape(height, breadth),
    )
    parts = back.reshape(n_grp, SIDE, shard, height + QB)
    dx_quant = jnp.swapaxes(parts[..., :height], 1, 2).reshape(n_grp, 1, shard, width)
    dx_scale = jnp.swapaxes(parts[..., height : height + height // QB], 1, 2)
    return (
        dx_quant,
        dx_scale.reshape(n_grp, 1, shard, width // QB),
        dw_quant[None, None],
        dw_scale[None, None],
    )


def solution(mesh):
    return jax.shard_map(
        on_device,
        mesh=mesh,
        in_specs=(
            P(None, "grp", "grid", None),
            P(None, "grp", "grid", None),
            P(None, "grp", "grid", None),
            P("grp", "grid", None, None),
            P(),
        ),
        out_specs=(
            P(None, "grp", "grid", None),
            P(None, "grp", "grid", None),
            P("grp", "grid", None, None),
            P("grp", "grid", None, None),
        ),
        check_vma=False,
    )
```

```python
import functools

import jax
import jax.numpy as jnp
from jax import lax
from jax.experimental import pallas as pl
from jax.experimental.pallas import tpu as pltpu
from jax.sharding import PartitionSpec as P

QB = 128
EPS = 1e-06
SIDE = 4
ORDER = (0, 1, 3, 2)

STEPS = (
    ("grad", 3),
    ("tokens", 1),
    ("tokens", 2),
    ("tokens", 3),
    ("tokens", 0),
    ("grad", 1),
    ("grad", 2),
    ("grad", 0),
    ("turn", ),
    ("grad_own", 3),
    ("dx", 0, 3),
    ("tokens_own", 1),
    ("tokens_own", 2),
    ("tokens_own", 3),
    ("tokens_own", 0),
    ("grad_own", 1),
    ("dx", 0, 1),
    ("tokens_near", 1),
    ("grad_own", 2),
    ("dx", 0, 2),
    ("tokens_near", 2),
    ("grad_own", 0),
    ("dx", 0, 0),
    ("tokens_near", 3),
    ("reduce", 0),
    ("grad_near", 3),
    ("grad_on", 3),
    ("dx", 1, 3),
    ("dx", 2, 3),
    ("tokens_near", 0),
    ("grad_near", 1),
    ("grad_on", 1),
    ("dx", 1, 1),
    ("dx", 2, 1),
    ("grad_near", 2),
    ("grad_on", 2),
    ("dx", 1, 2),
    ("dx", 2, 2),
    ("grad_near", 0),
    ("grad_on", 0),
    ("dx", 1, 0),
    ("dx", 2, 0),
    ("grad_far", 3),
    ("dx", 3, 3),
    ("tokens_far", 1),
    ("tokens_far", 2),
    ("tokens_far", 3),
    ("tokens_far", 0),
    ("turn_tokens", 0),
    ("turn_tokens", 1),
    ("turn_tokens", 2),
    ("turn_tokens", 3),
    ("dw", 0, True, False),
    ("reduce", 1),
    ("reduce", 2),
    ("grad_far", 1),
    ("dx", 3, 1),
    ("grad_far", 2),
    ("dx", 3, 2),
    ("grad_far", 0),
    ("dx", 3, 0),
    ("dw", 1, False, False),
    ("reduce", 3),
    ("dw", 2, False, False),
    ("dw", 3, False, True),
)
MESH = pl.DeviceIdType.MESH
F32 = jnp.float32
BF16 = jnp.bfloat16


def kernel(
    sizes,
    counts,
    scale,
    dy,
    tokens,
    weight,
    back,
    dw_out,
    dw_scale,
    dy_in,
    grad,
    w_in,
    w_t,
    g_all,
    t_all,
    rs_send,
    rs_half,
    rs_recv,
    own_sum,
    back_send,
    dw_sum,
    dw_quant,
    load_sem,
    g_send,
    g_recv,
    t_send,
    t_recv,
    z_send,
    z_recv,
    y_send,
    y_recv,
    h_send,
    h_recv,
    r_send,
    r_recv,
    b_send,
    b_recv,
    out_sem,
):
    n_grp, shard, height, breadth = sizes
    nx = n_grp // 2
    chunk = n_grp * shard
    block = SIDE * chunk
    g = lax.axis_index("grp")
    t = lax.axis_index("grid")
    x = g // 2
    c = g % 2
    z = t // SIDE
    y = t % SIDE

    def grp_at(dx, dc):
        return ((x + dx) % nx) * 2 + (c + dc) % 2

    def z_at(d):
        return (z + d + SIDE) % SIDE

    def y_at(d):
        return (y + d + SIDE) % SIDE

    x_order = []
    for near in range(1, nx // 2 + 1):
        for dc in range(2):
            x_order.append((near, dc))
            if nx - near != near:
                x_order.append((nx - near, dc))
    x_order += [(0, 1), (0, 0)]

    load_dy = pltpu.make_async_copy(dy, dy_in, load_sem.at[0])
    load_w = pltpu.make_async_copy(weight, w_in, load_sem.at[1])
    load_dy.start()
    load_w.start()

    barrier = pltpu.get_barrier_semaphore()
    partners = 0
    for dx, dc in x_order:
        for d in range(SIDE):
            if (dx, dc, d) != (0, 0, 0):
                pl.semaphore_signal(
                    barrier, inc=1, device_id=(grp_at(dx, dc), z * SIDE + y_at(d)), device_id_type=MESH
                )
                partners += 1
            if d != 0:
                pl.semaphore_signal(
                    barrier, inc=1, device_id=(grp_at(dx, dc), z_at(d) * SIDE + y), device_id_type=MESH
                )
                partners += 1

    load_dy.wait()
    groups = dy_in.shape[1] // QB

    def dequantize(e, carry):
        rows = pl.ds(pl.multiple_of(e * shard, shard), shard)
        live = t * shard + lax.broadcasted_iota(jnp.int32, (shard, groups), 0) < counts[g, e]
        s = jnp.where(live, scale[rows, :].astype(F32), 0.0)
        for j in range(groups):
            cols = slice(j * QB, (j + 1) * QB)
            grad[rows, cols] = (dy_in[rows, cols].astype(F32) * s[:, j : j + 1]).astype(BF16)
        return carry

    lax.fori_loop(0, n_grp, dequantize, 0)
    pl.semaphore_wait(barrier, partners)

    mine = pl.ds(pl.multiple_of(t * chunk + g * shard, shard), shard)
    waits = []

    def remote(src, dst, send, recv, device, to=None):
        copy = pltpu.make_async_remote_copy(
            src_ref=src, dst_ref=dst, send_sem=send, recv_sem=recv, device_id=device, device_id_type=MESH
        )
        copy.start()
        (waits if to is None else to).append(copy)

    in_flight = {}

    def send_grad(index):
        d = ORDER[index]
        b = y_at(d)
        sent = in_flight["grad", index] = []
        cols = pl.ds(pl.multiple_of(b * breadth, breadth), breadth)
        for i, (dx, dc) in enumerate(x_order):
            e = grp_at(dx, dc)
            src = grad.at[pl.ds(pl.multiple_of(e * shard, shard), shard), cols]
            if (dx, dc, d) == (0, 0, 0):
                pltpu.make_async_copy(src, g_all.at[mine, :], g_recv.at[y]).start()
            else:
                remote(
                    src, g_all.at[mine, :], g_send.at[index * n_grp + i], g_recv.at[y], (e, z * SIDE + b), sent
                )

    def send_tokens(index):
        d = ORDER[index]
        a = z_at(d)
        sent = in_flight["tokens", index] = []
        cols = pl.ds(pl.multiple_of(a * height, height), height)
        for i, (dx, dc) in enumerate(x_order):
            e = grp_at(dx, dc)
            src = tokens.at[pl.ds(pl.multiple_of(e * shard, shard), shard), cols]
            if (dx, dc, d) == (0, 0, 0):
                pltpu.make_async_copy(src, t_all.at[mine, :], t_recv.at[z]).start()
            else:
                remote(
                    src, t_all.at[mine, :], t_send.at[index * n_grp + i], t_recv.at[z], (e, a * SIDE + y), sent
                )

    def sent(name, index):
        for copy in in_flight.pop((name, index)):
            copy.wait_send()

    step = 256

    def turn(i, carry):
        rows = pl.ds(pl.multiple_of(i * step, step), step)
        for j in range(height // step):
            w_t[rows, j * step : (j + 1) * step] = w_in[j * step : (j + 1) * step, rows].T
        return carry

    def turn_weight():
        load_w.wait()
        lax.fori_loop(0, breadth // step, turn, 0)

    def rows_of(zs, ys):
        return pl.ds(pl.multiple_of((zs * SIDE + ys) * chunk, chunk), chunk)

    def landed(ref, sem):
        pltpu.make_async_copy(ref, ref, sem).wait()

    def cut_of(kz):
        return (3 if kz in (0, 3) else 2) * step

    def cut_of(kz):
        return (3 if kz in (0, 3) else 2) * step

    def input_gradient(kz, k):
        cut = cut_of(kz)
        halves = {1: slice(cut, height), 2: slice(0, cut)}
        p = jnp.dot(g_all[rows_of(z_at(ORDER[kz]), y_at(ORDER[k])), :], w_t[...], preferred_element_type=F32)
        if k == 0:
            own_sum[kz] = p
            return
        slot = kz * 3 + k - 1
        src = rs_send.at[slot]
        if k == 3:
            rs_send[slot] = p.astype(BF16)
            for way, d in ((0, 3), (1, 1)):
                cols = halves[2 - way]
                sem = kz * 2 + way
                remote(
                    src.at[:, cols],
                    rs_half.at[kz, :, cols],
                    h_send.at[sem],
                    h_recv.at[sem],
                    (g, z * SIDE + y_at(d)),
                )
            return
        other = halves[3 - k]
        cols = halves[k]
        rs_send[slot, :, other] = p[:, other].astype(BF16)
        landed(rs_half.at[kz, :, cols], h_recv.at[kz * 2 + k % 2])
        rs_send[slot, :, cols] = (p[:, cols] + rs_half[kz, :, cols].astype(F32)).astype(BF16)
        slot = kz * 2 + k - 1
        remote(src, rs_recv.at[slot], r_send.at[slot], r_recv.at[slot], (g, z * SIDE + y_at(ORDER[k])))

    def reduce(kz):
        for slot in (kz * 2, kz * 2 + 1):
            landed(rs_recv.at[slot], r_recv.at[slot])
        half = 16

        def part(i, carry):
            rows = pl.ds(pl.multiple_of(i * half, half), half)
            lanes = lax.broadcasted_iota(jnp.int32, (half, QB), 1)
            scales = jnp.zeros((half, QB), F32)
            for j in range(height // QB):
                cols = slice(j * QB, (j + 1) * QB)
                total = own_sum[kz, rows, cols]
                for slot in (kz * 2, kz * 2 + 1):
                    total = total + rs_recv[slot, rows, cols].astype(F32)
                s = jnp.max(jnp.abs(total), axis=1, keepdims=True) + EPS
                back_send[kz, rows, cols] = (total * (1.0 / s)).astype(BF16)
                scales = jnp.where(lanes == j, s, scales)
            back_send[kz, rows, height:] = scales.astype(BF16)
            return carry

        lax.fori_loop(0, chunk // half, part, 0)
        zs = z_at(ORDER[kz])
        dst = back.at[pl.ds(pl.multiple_of((g * SIDE + z) * shard, shard), shard), :]
        for i, (dx, dc) in enumerate(x_order):
            r = grp_at(dx, dc)
            src = back_send.at[kz, pl.ds(pl.multiple_of(r * shard, shard), shard), :]
            if (dx, dc, kz) == (0, 0, 0):
                pltpu.make_async_copy(src, dst, b_recv).start()
            else:
                remote(src, dst, b_send.at[kz * n_grp + i], b_recv, (r, zs * SIDE + y))

    wide = 512

    def turn_tokens(kz):
        for u in range(block // step):
            rows = pl.ds(pl.multiple_of(z_at(ORDER[kz]) * block + u * step, step), step)

            def turn(i, carry):
                down = pl.ds(pl.multiple_of(i * step, step), step)
                w_in[down, rows] = t_all[rows, down].T
                return carry

            lax.fori_loop(0, height // step, turn, 0)

    def weight_gradient(kz, first, last):
        rows = pl.ds(pl.multiple_of(z_at(ORDER[kz]) * block, block), block)

        def col_step(j, carry):
            along = pl.ds(pl.multiple_of(j * wide, wide), wide)
            p = jnp.dot(w_in[:, rows], g_all[rows, along], preferred_element_type=F32)
            if not first:
                p = p + dw_sum[:, along]
            if not last:
                dw_sum[:, along] = p
                return carry
            at_row = lax.broadcasted_iota(jnp.int32, dw_scale.shape, 0)
            at_col = lax.broadcasted_iota(jnp.int32, dw_scale.shape, 1)
            scales = dw_scale[...]
            for u in range(height // QB):
                for v in range(wide // QB):
                    q = p[u * QB : (u + 1) * QB, v * QB : (v + 1) * QB]
                    s = jnp.max(jnp.max(jnp.abs(q), axis=0, keepdims=True), axis=1, keepdims=True) + EPS
                    cols = pl.ds(pl.multiple_of(j * wide + v * QB, QB), QB)
                    dw_quant[u * QB : (u + 1) * QB, cols] = (q * (1.0 / s)).astype(BF16)
                    scales = jnp.where((at_row == u) & (at_col == j * (wide // QB) + v), s, scales)
            dw_scale[...] = scales
            pltpu.make_async_copy(dw_quant.at[:, along], dw_out.at[:, along], out_sem.at[j]).start()
            return carry

        lax.fori_loop(0, breadth // wide, col_step, 0)

    def half_of(zs, ys, upper):
        start = (zs * SIDE + ys) * chunk + (chunk // 2 if upper else 0)
        return pl.ds(pl.multiple_of(start, chunk // 2), chunk // 2)

    def pass_on(buffer, rows, send, recv, device):
        remote(buffer.at[rows, :], buffer.at[rows, :], send, recv, device)

    def grad_own(k):
        rows = rows_of(z, y_at(ORDER[k]))
        landed(g_all.at[rows, :], g_recv.at[y_at(ORDER[k])])
        for way, d in enumerate((1, 3)):
            sem = way * SIDE + k
            pass_on(g_all, rows, z_send.at[sem], z_recv.at[sem], (g, z_at(d) * SIDE + y))

    def grad_near(k):
        for way, d in enumerate((1, 3)):
            landed(g_all.at[rows_of(z_at(-d), y_at(ORDER[k])), :], z_recv.at[way * SIDE + k])

    def grad_on(k):
        for way, d in enumerate((1, 3)):
            rows = half_of(z_at(-d), y_at(ORDER[k]), way == 0)
            sem = (2 + way) * SIDE + k
            pass_on(g_all, rows, z_send.at[sem], z_recv.at[sem], (g, z_at(d) * SIDE + y))

    def grad_far(k):
        for way in range(2):
            rows = half_of(z_at(2), y_at(ORDER[k]), way == 0)
            landed(g_all.at[rows, :], z_recv.at[(2 + way) * SIDE + k])

    def tokens_own(k):
        rows = rows_of(z_at(ORDER[k]), y)
        landed(t_all.at[rows, :], t_recv.at[z_at(ORDER[k])])
        for way, d in enumerate((1, 3)):
            sem = way * SIDE + k
            pass_on(t_all, rows, y_send.at[sem], y_recv.at[sem], (g, z * SIDE + y_at(d)))

    def tokens_near(k):
        for way, d in enumerate((1, 3)):
            landed(t_all.at[rows_of(z_at(ORDER[k]), y_at(-d)), :], y_recv.at[way * SIDE + k])
            rows = half_of(z_at(ORDER[k]), y_at(-d), way == 0)
            sem = (2 + way) * SIDE + k
            pass_on(t_all, rows, y_send.at[sem], y_recv.at[sem], (g, z * SIDE + y_at(d)))

    def tokens_far(k):
        for way in range(2):
            rows = half_of(z_at(ORDER[k]), y_at(2), way == 0)
            landed(t_all.at[rows, :], y_recv.at[(2 + way) * SIDE + k])

    dw_scale[...] = jnp.zeros(dw_scale.shape, F32)
    actions = {
        "grad": send_grad,
        "tokens": send_tokens,
        "grad_sent": functools.partial(sent, "grad"),
        "tokens_sent": functools.partial(sent, "tokens"),
        "turn": turn_weight,
        "grad_own": grad_own,
        "grad_near": grad_near,
        "grad_on": grad_on,
        "turn_tokens": turn_tokens,
        "grad_far": grad_far,
        "tokens_own": tokens_own,
        "tokens_near": tokens_near,
        "tokens_far": tokens_far,
        "dx": input_gradient,
        "reduce": reduce,
        "dw": weight_gradient,
    }
    for name, *numbers in STEPS:
        actions[name](*numbers)

    for j in range(breadth // wide):
        along = pl.ds(j * wide, wide)
        pltpu.make_async_copy(dw_quant.at[:, along], dw_out.at[:, along], out_sem.at[j]).wait()
    for copy in sum(in_flight.values(), waits):
        copy.wait_send()
    landed(back, b_recv)


def on_device(dy_quant, dy_scale, tokens, weight, counts):
    n_grp, _, shard, hidden = dy_quant.shape
    width = tokens.shape[-1]
    height, breadth = weight.shape[-2:]
    rows = n_grp * shard
    slots = SIDE * SIDE * rows
    dma = pltpu.SemaphoreType.DMA
    back, dw_quant, dw_scale = pl.pallas_call(
        functools.partial(kernel, (n_grp, shard, height, breadth)),
        out_shape=(
            jax.ShapeDtypeStruct((n_grp * SIDE * shard, height + QB), BF16),
            jax.ShapeDtypeStruct((height, breadth), BF16),
            jax.ShapeDtypeStruct((height // QB, breadth // QB), F32),
        ),
        in_specs=[
            pl.BlockSpec(memory_space=pltpu.SMEM),
            pl.BlockSpec(memory_space=pltpu.VMEM),
            pl.BlockSpec(memory_space=pl.ANY),
            pl.BlockSpec(memory_space=pl.ANY),
            pl.BlockSpec(memory_space=pl.ANY),
        ],
        out_specs=(
            pl.BlockSpec(memory_space=pl.ANY),
            pl.BlockSpec(memory_space=pl.ANY),
            pl.BlockSpec(memory_space=pltpu.VMEM),
        ),
        scratch_shapes=[
            pltpu.VMEM((rows, hidden), BF16),
            pltpu.VMEM((rows, hidden), BF16),
            pltpu.VMEM((height, breadth), BF16),
            pltpu.VMEM((breadth, height), BF16),
            pltpu.VMEM((slots, breadth), BF16),
            pltpu.VMEM((slots, height), BF16),
            pltpu.VMEM((12, rows, height), BF16),
            pltpu.VMEM((SIDE, rows, height), BF16),
            pltpu.VMEM((8, rows, height), BF16),
            pltpu.VMEM((SIDE, rows, height), F32),
            pltpu.VMEM((SIDE, rows, height + QB), BF16),
            pltpu.VMEM((height, breadth), F32),
            pltpu.VMEM((height, breadth), BF16),
            dma((2,)),
            dma((SIDE * n_grp,)),
            dma((SIDE,)),
            dma((SIDE * n_grp,)),
            dma((SIDE,)),
            dma((16,)),
            dma((16,)),
            dma((16,)),
            dma((16,)),
            dma((8,)),
            dma((8,)),
            dma((8,)),
            dma((8,)),
            dma((SIDE * n_grp,)),
            dma,
            dma((breadth // 512,)),
        ],
        compiler_params=pltpu.CompilerParams(
            collective_id=0, has_side_effects=True, vmem_limit_bytes=62 * 2**20
        ),
        name="up_backward",
    )(
        counts,
        dy_scale.reshape(rows, hidden // QB),
        dy_quant.reshape(rows, hidden),
        tokens.reshape(rows, width),
        weight.reshape(height, breadth),
    )
    dx_quant, dx_scale, dw_quant = finish(
        back.reshape(n_grp, SIDE, shard, height + QB), dw_quant
    )
    return (dx_quant[:, None], dx_scale[:, None], dw_quant[None, None], dw_scale[None, None])


def finish_kernel(back, dw, dx_out, scale_out, dw_out, scales, dx, dw_in, scale_sem, dx_sem, dw_sem):
    n_grp, parts, shard, width = back.shape
    height = width - QB
    groups = height // QB
    loads = []
    for a in range(parts):
        cols = slice(a * height, (a + 1) * height)
        loads.append(pltpu.make_async_copy(back.at[:, a, :, :height], dx.at[:, :, cols], dx_sem.at[0, a]))
    piece = dw.shape[0] // dw_sem.shape[1]
    for i in range(dw_sem.shape[1]):
        rows = slice(i * piece, (i + 1) * piece)
        loads.append(pltpu.make_async_copy(dw.at[rows], dw_in.at[rows], dw_sem.at[0, i]))
    load = pltpu.make_async_copy(back.at[:, :, :, height:], scales, scale_sem)
    for copy in loads:
        copy.start()
    load.start()
    copies = []
    for a in range(parts):
        loads[a].wait()
    for a in range(2):
        part = slice(a * n_grp // 2, (a + 1) * n_grp // 2)
        copies.append(pltpu.make_async_copy(dx.at[part], dx_out.at[part], dx_sem.at[1, a]))
        copies[-1].start()
    for i in range(dw_sem.shape[1]):
        loads[parts + i].wait()
        rows = slice(i * piece, (i + 1) * piece)
        copies.append(pltpu.make_async_copy(dw_in.at[rows], dw_out.at[rows], dw_sem.at[1, i]))
        copies[-1].start()
    load.wait()
    for e in range(n_grp):
        line = [scales[e, a][:, :groups] for a in range(parts)]
        scale_out[e] = jnp.concatenate(line, axis=1)
    for copy in copies:
        copy.wait()


def finish(back, dw):
    n_grp, parts, shard, width = back.shape
    height = width - QB
    anywhere = pl.BlockSpec(memory_space=pl.ANY)
    dma = pltpu.SemaphoreType.DMA
    return pl.pallas_call(
        finish_kernel,
        out_shape=(
            jax.ShapeDtypeStruct((n_grp, shard, parts * height), BF16),
            jax.ShapeDtypeStruct((n_grp, shard, parts * height // QB), BF16),
            jax.ShapeDtypeStruct(dw.shape, BF16),
        ),
        in_specs=[anywhere, anywhere],
        out_specs=(anywhere, pl.BlockSpec(memory_space=pltpu.VMEM), anywhere),
        scratch_shapes=[
            pltpu.VMEM((n_grp, parts, shard, QB), BF16),
            pltpu.VMEM((n_grp, shard, parts * height), BF16),
            pltpu.VMEM(dw.shape, BF16),
            dma,
            dma((2, parts)),
            dma((2, 5)),
        ],
        compiler_params=pltpu.CompilerParams(vmem_limit_bytes=62 * 2**20),
        name="finish",
    )(back, dw)


def solution(mesh):
    return jax.shard_map(
        on_device,
        mesh=mesh,
        in_specs=(
            P(None, "grp", "grid", None),
            P(None, "grp", "grid", None),
            P(None, "grp", "grid", None),
            P("grp", "grid", None, None),
            P(),
        ),
        out_specs=(
            P(None, "grp", "grid", None),
            P(None, "grp", "grid", None),
            P("grp", "grid", None, None),
            P("grp", "grid", None, None),
        ),
        check_vma=False,
    )
```

```python
import functools

import jax
import jax.numpy as jnp
from jax import lax
from jax.experimental import pallas as pl
from jax.experimental.pallas import tpu as pltpu
from jax.sharding import PartitionSpec as P

QB = 128
EPS = 1e-06
SIDE = 4
ORDER = (0, 1, 3, 2)

STEPS = (
    ("grad", 3),
    ("tokens", 1),
    ("tokens", 2),
    ("grad", 1),
    ("grad", 2),
    ("tokens", 3),
    ("tokens", 0),
    ("grad", 0),
    ("turn", ),
    ("grad_own", 3),
    ("dx", 0, 3),
    ("tokens_own", 1),
    ("tokens_own", 2),
    ("grad_own", 1),
    ("dx", 0, 1),
    ("grad_own", 2),
    ("dx", 0, 2),
    ("grad_own", 0),
    ("dx", 0, 0),
    ("tokens_own", 3),
    ("tokens_own", 0),
    ("reduce", 0),
    ("grad_near", 3),
    ("grad_on", 3),
    ("dx", 1, 3),
    ("dx", 2, 3),
    ("tokens_near", 1),
    ("grad_near", 1),
    ("grad_on", 1),
    ("dx", 1, 1),
    ("dx", 2, 1),
    ("tokens_near", 2),
    ("grad_near", 2),
    ("grad_on", 2),
    ("dx", 1, 2),
    ("dx", 2, 2),
    ("grad_near", 0),
    ("grad_on", 0),
    ("dx", 1, 0),
    ("dx", 2, 0),
    ("grad_far", 3),
    ("dx", 3, 3),
    ("reduce", 1),
    ("reduce", 2),
    ("grad_far", 1),
    ("dx", 3, 1),
    ("grad_far", 2),
    ("dx", 3, 2),
    ("tokens_near", 3),
    ("tokens_near", 0),
    ("tokens_far", 1),
    ("turn_tokens", 1),
    ("dw", 1, True, False),
    ("grad_far", 0),
    ("dx", 3, 0),
    ("tokens_far", 2),
    ("turn_tokens", 2),
    ("dw", 2, False, False),
    ("reduce", 3),
    ("tokens_far", 3),
    ("turn_tokens", 3),
    ("dw", 3, False, False),
    ("tokens_far", 0),
    ("turn_tokens", 0),
    ("dw", 0, False, True),
)
MESH = pl.DeviceIdType.MESH
F32 = jnp.float32
BF16 = jnp.bfloat16


def kernel(
    sizes,
    counts,
    scale,
    dy,
    tokens,
    weight,
    back,
    dw_out,
    dw_scale,
    dy_in,
    grad,
    w_in,
    w_t,
    g_all,
    t_all,
    rs_send,
    rs_half,
    rs_recv,
    own_sum,
    back_send,
    dw_sum,
    dw_quant,
    load_sem,
    g_send,
    g_recv,
    t_send,
    t_recv,
    z_send,
    z_recv,
    y_send,
    y_recv,
    h_send,
    h_recv,
    r_send,
    r_recv,
    b_send,
    b_recv,
    out_sem,
):
    n_grp, shard, height, breadth = sizes
    nx = n_grp // 2
    chunk = n_grp * shard
    block = SIDE * chunk
    g = lax.axis_index("grp")
    t = lax.axis_index("grid")
    x = g // 2
    c = g % 2
    z = t // SIDE
    y = t % SIDE

    def grp_at(dx, dc):
        return ((x + dx) % nx) * 2 + (c + dc) % 2

    def z_at(d):
        return (z + d + SIDE) % SIDE

    def y_at(d):
        return (y + d + SIDE) % SIDE

    x_order = []
    for near in range(1, nx // 2 + 1):
        for dc in range(2):
            x_order.append((near, dc))
            if nx - near != near:
                x_order.append((nx - near, dc))
    x_order += [(0, 1), (0, 0)]

    load_dy = pltpu.make_async_copy(dy, dy_in, load_sem.at[0])
    load_w = pltpu.make_async_copy(weight, w_in, load_sem.at[1])
    load_dy.start()
    load_w.start()

    barrier = pltpu.get_barrier_semaphore()
    partners = 0
    for dx, dc in x_order:
        for d in range(SIDE):
            if (dx, dc, d) != (0, 0, 0):
                pl.semaphore_signal(
                    barrier, inc=1, device_id=(grp_at(dx, dc), z * SIDE + y_at(d)), device_id_type=MESH
                )
                partners += 1
            if d != 0:
                pl.semaphore_signal(
                    barrier, inc=1, device_id=(grp_at(dx, dc), z_at(d) * SIDE + y), device_id_type=MESH
                )
                partners += 1

    load_dy.wait()
    groups = dy_in.shape[1] // QB

    def dequantize(e, carry):
        rows = pl.ds(pl.multiple_of(e * shard, shard), shard)
        live = t * shard + lax.broadcasted_iota(jnp.int32, (shard, groups), 0) < counts[g, e]
        s = jnp.where(live, scale[rows, :].astype(F32), 0.0)
        for j in range(groups):
            cols = slice(j * QB, (j + 1) * QB)
            grad[rows, cols] = (dy_in[rows, cols].astype(F32) * s[:, j : j + 1]).astype(BF16)
        return carry

    lax.fori_loop(0, n_grp, dequantize, 0)
    pl.semaphore_wait(barrier, partners)

    mine = pl.ds(pl.multiple_of(t * chunk + g * shard, shard), shard)
    waits = []

    def remote(src, dst, send, recv, device, to=None):
        copy = pltpu.make_async_remote_copy(
            src_ref=src, dst_ref=dst, send_sem=send, recv_sem=recv, device_id=device, device_id_type=MESH
        )
        copy.start()
        (waits if to is None else to).append(copy)

    in_flight = {}

    def send_grad(index):
        d = ORDER[index]
        b = y_at(d)
        sent = in_flight["grad", index] = []
        cols = pl.ds(pl.multiple_of(b * breadth, breadth), breadth)
        for i, (dx, dc) in enumerate(x_order):
            e = grp_at(dx, dc)
            src = grad.at[pl.ds(pl.multiple_of(e * shard, shard), shard), cols]
            if (dx, dc, d) == (0, 0, 0):
                pltpu.make_async_copy(src, g_all.at[mine, :], g_recv.at[y]).start()
            else:
                remote(
                    src, g_all.at[mine, :], g_send.at[index * n_grp + i], g_recv.at[y], (e, z * SIDE + b), sent
                )

    def send_tokens(index):
        d = ORDER[index]
        a = z_at(d)
        sent = in_flight["tokens", index] = []
        cols = pl.ds(pl.multiple_of(a * height, height), height)
        for i, (dx, dc) in enumerate(x_order):
            e = grp_at(dx, dc)
            src = tokens.at[pl.ds(pl.multiple_of(e * shard, shard), shard), cols]
            if (dx, dc, d) == (0, 0, 0):
                pltpu.make_async_copy(src, t_all.at[mine, :], t_recv.at[z]).start()
            else:
                remote(
                    src, t_all.at[mine, :], t_send.at[index * n_grp + i], t_recv.at[z], (e, a * SIDE + y), sent
                )

    def sent(name, index):
        for copy in in_flight.pop((name, index)):
            copy.wait_send()

    step = 256

    def turn(i, carry):
        rows = pl.ds(pl.multiple_of(i * step, step), step)
        for j in range(height // step):
            w_t[rows, j * step : (j + 1) * step] = w_in[j * step : (j + 1) * step, rows].T
        return carry

    def turn_weight():
        load_w.wait()
        lax.fori_loop(0, breadth // step, turn, 0)

    def rows_of(zs, ys):
        return pl.ds(pl.multiple_of((zs * SIDE + ys) * chunk, chunk), chunk)

    def landed(ref, sem):
        pltpu.make_async_copy(ref, ref, sem).wait()

    def cut_of(kz):
        return (3 if kz in (0, 3) else 2) * step

    def cut_of(kz):
        return (3 if kz in (0, 3) else 2) * step

    def input_gradient(kz, k):
        cut = cut_of(kz)
        halves = {1: slice(cut, height), 2: slice(0, cut)}
        p = jnp.dot(g_all[rows_of(z_at(ORDER[kz]), y_at(ORDER[k])), :], w_t[...], preferred_element_type=F32)
        if k == 0:
            own_sum[kz] = p
            return
        slot = kz * 3 + k - 1
        src = rs_send.at[slot]
        if k == 3:
            rs_send[slot] = p.astype(BF16)
            for way, d in ((0, 3), (1, 1)):
                cols = halves[2 - way]
                sem = kz * 2 + way
                remote(
                    src.at[:, cols],
                    rs_half.at[kz, :, cols],
                    h_send.at[sem],
                    h_recv.at[sem],
                    (g, z * SIDE + y_at(d)),
                )
            return
        other = halves[3 - k]
        cols = halves[k]
        rs_send[slot, :, other] = p[:, other].astype(BF16)
        landed(rs_half.at[kz, :, cols], h_recv.at[kz * 2 + k % 2])
        rs_send[slot, :, cols] = (p[:, cols] + rs_half[kz, :, cols].astype(F32)).astype(BF16)
        slot = kz * 2 + k - 1
        remote(src, rs_recv.at[slot], r_send.at[slot], r_recv.at[slot], (g, z * SIDE + y_at(ORDER[k])))

    def reduce(kz):
        for slot in (kz * 2, kz * 2 + 1):
            landed(rs_recv.at[slot], r_recv.at[slot])
        half = 16

        def part(i, carry):
            rows = pl.ds(pl.multiple_of(i * half, half), half)
            lanes = lax.broadcasted_iota(jnp.int32, (half, QB), 1)
            scales = jnp.zeros((half, QB), F32)
            for j in range(height // QB):
                cols = slice(j * QB, (j + 1) * QB)
                total = own_sum[kz, rows, cols]
                for slot in (kz * 2, kz * 2 + 1):
                    total = total + rs_recv[slot, rows, cols].astype(F32)
                s = jnp.max(jnp.abs(total), axis=1, keepdims=True) + EPS
                back_send[kz, rows, cols] = (total * (1.0 / s)).astype(BF16)
                scales = jnp.where(lanes == j, s, scales)
            back_send[kz, rows, height:] = scales.astype(BF16)
            return carry

        lax.fori_loop(0, chunk // half, part, 0)
        zs = z_at(ORDER[kz])
        dst = back.at[pl.ds(pl.multiple_of((g * SIDE + z) * shard, shard), shard), :]
        for i, (dx, dc) in enumerate(x_order):
            r = grp_at(dx, dc)
            src = back_send.at[kz, pl.ds(pl.multiple_of(r * shard, shard), shard), :]
            if (dx, dc, kz) == (0, 0, 0):
                pltpu.make_async_copy(src, dst, b_recv).start()
            else:
                remote(src, dst, b_send.at[kz * n_grp + i], b_recv, (r, zs * SIDE + y))

    wide = 512

    def turn_tokens(kz):
        for u in range(block // step):
            rows = pl.ds(pl.multiple_of(z_at(ORDER[kz]) * block + u * step, step), step)

            def turn(i, carry):
                down = pl.ds(pl.multiple_of(i * step, step), step)
                w_in[down, rows] = t_all[rows, down].T
                return carry

            lax.fori_loop(0, height // step, turn, 0)

    def weight_gradient(kz, first, last):
        rows = pl.ds(pl.multiple_of(z_at(ORDER[kz]) * block, block), block)

        def col_step(j, carry):
            along = pl.ds(pl.multiple_of(j * wide, wide), wide)
            p = jnp.dot(w_in[:, rows], g_all[rows, along], preferred_element_type=F32)
            if not first:
                p = p + dw_sum[:, along]
            if not last:
                dw_sum[:, along] = p
                return carry
            at_row = lax.broadcasted_iota(jnp.int32, dw_scale.shape, 0)
            at_col = lax.broadcasted_iota(jnp.int32, dw_scale.shape, 1)
            scales = dw_scale[...]
            for u in range(height // QB):
                for v in range(wide // QB):
                    q = p[u * QB : (u + 1) * QB, v * QB : (v + 1) * QB]
                    s = jnp.max(jnp.max(jnp.abs(q), axis=0, keepdims=True), axis=1, keepdims=True) + EPS
                    cols = pl.ds(pl.multiple_of(j * wide + v * QB, QB), QB)
                    dw_quant[u * QB : (u + 1) * QB, cols] = (q * (1.0 / s)).astype(BF16)
                    scales = jnp.where((at_row == u) & (at_col == j * (wide // QB) + v), s, scales)
            dw_scale[...] = scales
            pltpu.make_async_copy(dw_quant.at[:, along], dw_out.at[:, along], out_sem.at[j]).start()
            return carry

        lax.fori_loop(0, breadth // wide, col_step, 0)

    def half_of(zs, ys, upper):
        start = (zs * SIDE + ys) * chunk + (chunk // 2 if upper else 0)
        return pl.ds(pl.multiple_of(start, chunk // 2), chunk // 2)

    def pass_on(buffer, rows, send, recv, device):
        remote(buffer.at[rows, :], buffer.at[rows, :], send, recv, device)

    def grad_own(k):
        rows = rows_of(z, y_at(ORDER[k]))
        landed(g_all.at[rows, :], g_recv.at[y_at(ORDER[k])])
        for way, d in enumerate((1, 3)):
            sem = way * SIDE + k
            pass_on(g_all, rows, z_send.at[sem], z_recv.at[sem], (g, z_at(d) * SIDE + y))

    def grad_near(k):
        for way, d in enumerate((1, 3)):
            landed(g_all.at[rows_of(z_at(-d), y_at(ORDER[k])), :], z_recv.at[way * SIDE + k])

    def grad_on(k):
        for way, d in enumerate((1, 3)):
            rows = half_of(z_at(-d), y_at(ORDER[k]), way == 0)
            sem = (2 + way) * SIDE + k
            pass_on(g_all, rows, z_send.at[sem], z_recv.at[sem], (g, z_at(d) * SIDE + y))

    def grad_far(k):
        for way in range(2):
            rows = half_of(z_at(2), y_at(ORDER[k]), way == 0)
            landed(g_all.at[rows, :], z_recv.at[(2 + way) * SIDE + k])

    def tokens_own(k):
        rows = rows_of(z_at(ORDER[k]), y)
        landed(t_all.at[rows, :], t_recv.at[z_at(ORDER[k])])
        for way, d in enumerate((1, 3)):
            sem = way * SIDE + k
            pass_on(t_all, rows, y_send.at[sem], y_recv.at[sem], (g, z * SIDE + y_at(d)))

    def tokens_near(k):
        for way, d in enumerate((1, 3)):
            landed(t_all.at[rows_of(z_at(ORDER[k]), y_at(-d)), :], y_recv.at[way * SIDE + k])
            rows = half_of(z_at(ORDER[k]), y_at(-d), way == 0)
            sem = (2 + way) * SIDE + k
            pass_on(t_all, rows, y_send.at[sem], y_recv.at[sem], (g, z * SIDE + y_at(d)))

    def tokens_far(k):
        for way in range(2):
            rows = half_of(z_at(ORDER[k]), y_at(2), way == 0)
            landed(t_all.at[rows, :], y_recv.at[(2 + way) * SIDE + k])

    dw_scale[...] = jnp.zeros(dw_scale.shape, F32)
    actions = {
        "grad": send_grad,
        "tokens": send_tokens,
        "grad_sent": functools.partial(sent, "grad"),
        "tokens_sent": functools.partial(sent, "tokens"),
        "turn": turn_weight,
        "grad_own": grad_own,
        "grad_near": grad_near,
        "grad_on": grad_on,
        "turn_tokens": turn_tokens,
        "grad_far": grad_far,
        "tokens_own": tokens_own,
        "tokens_near": tokens_near,
        "tokens_far": tokens_far,
        "dx": input_gradient,
        "reduce": reduce,
        "dw": weight_gradient,
    }
    for name, *numbers in STEPS:
        actions[name](*numbers)

    for j in range(breadth // wide):
        along = pl.ds(j * wide, wide)
        pltpu.make_async_copy(dw_quant.at[:, along], dw_out.at[:, along], out_sem.at[j]).wait()
    for copy in sum(in_flight.values(), waits):
        copy.wait_send()
    landed(back, b_recv)


def on_device(dy_quant, dy_scale, tokens, weight, counts):
    n_grp, _, shard, hidden = dy_quant.shape
    width = tokens.shape[-1]
    height, breadth = weight.shape[-2:]
    rows = n_grp * shard
    slots = SIDE * SIDE * rows
    dma = pltpu.SemaphoreType.DMA
    back, dw_quant, dw_scale = pl.pallas_call(
        functools.partial(kernel, (n_grp, shard, height, breadth)),
        out_shape=(
            jax.ShapeDtypeStruct((n_grp * SIDE * shard, height + QB), BF16),
            jax.ShapeDtypeStruct((height, breadth), BF16),
            jax.ShapeDtypeStruct((height // QB, breadth // QB), F32),
        ),
        in_specs=[
            pl.BlockSpec(memory_space=pltpu.SMEM),
            pl.BlockSpec(memory_space=pltpu.VMEM),
            pl.BlockSpec(memory_space=pl.ANY),
            pl.BlockSpec(memory_space=pl.ANY),
            pl.BlockSpec(memory_space=pl.ANY),
        ],
        out_specs=(
            pl.BlockSpec(memory_space=pl.ANY),
            pl.BlockSpec(memory_space=pl.ANY),
            pl.BlockSpec(memory_space=pltpu.VMEM),
        ),
        scratch_shapes=[
            pltpu.VMEM((rows, hidden), BF16),
            pltpu.VMEM((rows, hidden), BF16),
            pltpu.VMEM((height, breadth), BF16),
            pltpu.VMEM((breadth, height), BF16),
            pltpu.VMEM((slots, breadth), BF16),
            pltpu.VMEM((slots, height), BF16),
            pltpu.VMEM((12, rows, height), BF16),
            pltpu.VMEM((SIDE, rows, height), BF16),
            pltpu.VMEM((8, rows, height), BF16),
            pltpu.VMEM((SIDE, rows, height), F32),
            pltpu.VMEM((SIDE, rows, height + QB), BF16),
            pltpu.VMEM((height, breadth), F32),
            pltpu.VMEM((height, breadth), BF16),
            dma((2,)),
            dma((SIDE * n_grp,)),
            dma((SIDE,)),
            dma((SIDE * n_grp,)),
            dma((SIDE,)),
            dma((16,)),
            dma((16,)),
            dma((16,)),
            dma((16,)),
            dma((8,)),
            dma((8,)),
            dma((8,)),
            dma((8,)),
            dma((SIDE * n_grp,)),
            dma,
            dma((breadth // 512,)),
        ],
        compiler_params=pltpu.CompilerParams(
            collective_id=0, has_side_effects=True, vmem_limit_bytes=62 * 2**20
        ),
        name="up_backward",
    )(
        counts,
        dy_scale.reshape(rows, hidden // QB),
        dy_quant.reshape(rows, hidden),
        tokens.reshape(rows, width),
        weight.reshape(height, breadth),
    )
    dx_quant, dx_scale, dw_quant = finish(
        back.reshape(n_grp, SIDE, shard, height + QB), dw_quant
    )
    return (dx_quant[:, None], dx_scale[:, None], dw_quant[None, None], dw_scale[None, None])


def finish_kernel(back, dw, dx_out, scale_out, dw_out, scales, dx, dw_in, scale_sem, dx_sem, dw_sem):
    n_grp, parts, shard, width = back.shape
    height = width - QB
    groups = height // QB
    loads = []
    for a in range(parts):
        cols = slice(a * height, (a + 1) * height)
        loads.append(pltpu.make_async_copy(back.at[:, a, :, :height], dx.at[:, :, cols], dx_sem.at[0, a]))
    piece = dw.shape[0] // dw_sem.shape[1]
    for i in range(dw_sem.shape[1]):
        rows = slice(i * piece, (i + 1) * piece)
        loads.append(pltpu.make_async_copy(dw.at[rows], dw_in.at[rows], dw_sem.at[0, i]))
    load = pltpu.make_async_copy(back.at[:, :, :, height:], scales, scale_sem)
    for copy in loads:
        copy.start()
    load.start()
    copies = []
    for a in range(parts):
        loads[a].wait()
    for a in range(2):
        part = slice(a * n_grp // 2, (a + 1) * n_grp // 2)
        copies.append(pltpu.make_async_copy(dx.at[part], dx_out.at[part], dx_sem.at[1, a]))
        copies[-1].start()
    for i in range(dw_sem.shape[1]):
        loads[parts + i].wait()
        rows = slice(i * piece, (i + 1) * piece)
        copies.append(pltpu.make_async_copy(dw_in.at[rows], dw_out.at[rows], dw_sem.at[1, i]))
        copies[-1].start()
    load.wait()
    for e in range(n_grp):
        line = [scales[e, a][:, :groups] for a in range(parts)]
        scale_out[e] = jnp.concatenate(line, axis=1)
    for copy in copies:
        copy.wait()


def finish(back, dw):
    n_grp, parts, shard, width = back.shape
    height = width - QB
    anywhere = pl.BlockSpec(memory_space=pl.ANY)
    dma = pltpu.SemaphoreType.DMA
    return pl.pallas_call(
        finish_kernel,
        out_shape=(
            jax.ShapeDtypeStruct((n_grp, shard, parts * height), BF16),
            jax.ShapeDtypeStruct((n_grp, shard, parts * height // QB), BF16),
            jax.ShapeDtypeStruct(dw.shape, BF16),
        ),
        in_specs=[anywhere, anywhere],
        out_specs=(anywhere, pl.BlockSpec(memory_space=pltpu.VMEM), anywhere),
        scratch_shapes=[
            pltpu.VMEM((n_grp, parts, shard, QB), BF16),
            pltpu.VMEM((n_grp, shard, parts * height), BF16),
            pltpu.VMEM(dw.shape, BF16),
            dma,
            dma((2, parts)),
            dma((2, 5)),
        ],
        compiler_params=pltpu.CompilerParams(vmem_limit_bytes=62 * 2**20),
        name="finish",
    )(back, dw)


def solution(mesh):
    return jax.shard_map(
        on_device,
        mesh=mesh,
        in_specs=(
            P(None, "grp", "grid", None),
            P(None, "grp", "grid", None),
            P(None, "grp", "grid", None),
            P("grp", "grid", None, None),
            P(),
        ),
        out_specs=(
            P(None, "grp", "grid", None),
            P(None, "grp", "grid", None),
            P("grp", "grid", None, None),
            P("grp", "grid", None, None),
        ),
        check_vma=False,
    )
```

```python
import functools

import jax
import jax.numpy as jnp
from jax import lax
from jax.experimental import pallas as pl
from jax.experimental.pallas import tpu as pltpu
from jax.sharding import PartitionSpec as P

QB = 128
EPS = 1e-06
SIDE = 4
ORDER = (0, 1, 3, 2)

STEPS = (
    ("grad", 3),
    ("tokens", 1),
    ("tokens", 2),
    ("grad", 1),
    ("grad", 2),
    ("tokens", 3),
    ("tokens", 0),
    ("grad", 0),
    ("turn", ),
    ("grad_own", 3),
    ("dx", 0, 3),
    ("tokens_own", 1),
    ("tokens_own", 2),
    ("grad_own", 1),
    ("dx", 0, 1),
    ("grad_own", 2),
    ("dx", 0, 2),
    ("grad_own", 0),
    ("dx", 0, 0),
    ("tokens_own", 3),
    ("tokens_own", 0),
    ("reduce", 0),
    ("grad_near", 3),
    ("grad_on", 3),
    ("dx", 1, 3),
    ("dx", 2, 3),
    ("tokens_near", 1),
    ("grad_near", 1),
    ("grad_on", 1),
    ("dx", 1, 1),
    ("dx", 2, 1),
    ("tokens_near", 2),
    ("grad_near", 2),
    ("grad_on", 2),
    ("dx", 1, 2),
    ("dx", 2, 2),
    ("grad_near", 0),
    ("grad_on", 0),
    ("dx", 1, 0),
    ("dx", 2, 0),
    ("grad_far", 3),
    ("dx", 3, 3),
    ("reduce", 1),
    ("reduce", 2),
    ("grad_far", 1),
    ("dx", 3, 1),
    ("grad_far", 2),
    ("dx", 3, 2),
    ("tokens_near", 3),
    ("tokens_near", 0),
    ("tokens_far", 1),
    ("turn_tokens", 1),
    ("dw", 1, True, False),
    ("grad_far", 0),
    ("dx", 3, 0),
    ("tokens_far", 2),
    ("turn_tokens", 2),
    ("dw", 2, False, False),
    ("reduce", 3),
    ("tokens_far", 3),
    ("turn_tokens", 3),
    ("dw", 3, False, False),
    ("tokens_far", 0),
    ("turn_tokens", 0),
    ("dw", 0, False, True),
)
MESH = pl.DeviceIdType.MESH
F32 = jnp.float32
BF16 = jnp.bfloat16


def kernel(
    sizes,
    counts,
    scale,
    dy,
    tokens,
    weight,
    back,
    dw_out,
    dw_scale,
    dy_in,
    grad,
    w_in,
    w_t,
    g_all,
    t_all,
    rs_send,
    rs_half,
    rs_recv,
    own_sum,
    back_send,
    dw_sum,
    dw_quant,
    load_sem,
    g_send,
    g_recv,
    t_send,
    t_recv,
    z_send,
    z_recv,
    y_send,
    y_recv,
    h_send,
    h_recv,
    r_send,
    r_recv,
    b_send,
    b_recv,
    out_sem,
):
    n_grp, shard, height, breadth = sizes
    nx = n_grp // 2
    chunk = n_grp * shard
    block = SIDE * chunk
    g = lax.axis_index("grp")
    t = lax.axis_index("grid")
    x = g // 2
    c = g % 2
    z = t // SIDE
    y = t % SIDE

    def grp_at(dx, dc):
        return ((x + dx) % nx) * 2 + (c + dc) % 2

    def z_at(d):
        return (z + d + SIDE) % SIDE

    def y_at(d):
        return (y + d + SIDE) % SIDE

    x_order = []
    for near in range(nx // 2, 0, -1):
        for dc in range(2):
            x_order.append((near, dc))
            if nx - near != near:
                x_order.append((nx - near, dc))
    x_order += [(0, 1), (0, 0)]

    load_dy = pltpu.make_async_copy(dy, dy_in, load_sem.at[0])
    load_w = pltpu.make_async_copy(weight, w_in, load_sem.at[1])
    load_dy.start()
    load_w.start()

    barrier = pltpu.get_barrier_semaphore()
    partners = 0
    for dx, dc in x_order:
        for d in range(SIDE):
            if (dx, dc, d) != (0, 0, 0):
                pl.semaphore_signal(
                    barrier, inc=1, device_id=(grp_at(dx, dc), z * SIDE + y_at(d)), device_id_type=MESH
                )
                partners += 1
            if d != 0:
                pl.semaphore_signal(
                    barrier, inc=1, device_id=(grp_at(dx, dc), z_at(d) * SIDE + y), device_id_type=MESH
                )
                partners += 1

    load_dy.wait()
    groups = dy_in.shape[1] // QB

    def dequantize(e, carry):
        rows = pl.ds(pl.multiple_of(e * shard, shard), shard)
        live = t * shard + lax.broadcasted_iota(jnp.int32, (shard, groups), 0) < counts[g, e]
        s = jnp.where(live, scale[rows, :].astype(F32), 0.0)
        for j in range(groups):
            cols = slice(j * QB, (j + 1) * QB)
            grad[rows, cols] = (dy_in[rows, cols].astype(F32) * s[:, j : j + 1]).astype(BF16)
        return carry

    lax.fori_loop(0, n_grp, dequantize, 0)
    pl.semaphore_wait(barrier, partners)

    mine = pl.ds(pl.multiple_of(t * chunk + g * shard, shard), shard)
    waits = []

    def remote(src, dst, send, recv, device, to=None):
        copy = pltpu.make_async_remote_copy(
            src_ref=src, dst_ref=dst, send_sem=send, recv_sem=recv, device_id=device, device_id_type=MESH
        )
        copy.start()
        (waits if to is None else to).append(copy)

    in_flight = {}

    def send_grad(index):
        d = ORDER[index]
        b = y_at(d)
        sent = in_flight["grad", index] = []
        cols = pl.ds(pl.multiple_of(b * breadth, breadth), breadth)
        for i, (dx, dc) in enumerate(x_order):
            e = grp_at(dx, dc)
            src = grad.at[pl.ds(pl.multiple_of(e * shard, shard), shard), cols]
            if (dx, dc, d) == (0, 0, 0):
                pltpu.make_async_copy(src, g_all.at[mine, :], g_recv.at[y]).start()
            else:
                remote(
                    src, g_all.at[mine, :], g_send.at[index * n_grp + i], g_recv.at[y], (e, z * SIDE + b), sent
                )

    def send_tokens(index):
        d = ORDER[index]
        a = z_at(d)
        sent = in_flight["tokens", index] = []
        cols = pl.ds(pl.multiple_of(a * height, height), height)
        for i, (dx, dc) in enumerate(x_order):
            e = grp_at(dx, dc)
            src = tokens.at[pl.ds(pl.multiple_of(e * shard, shard), shard), cols]
            if (dx, dc, d) == (0, 0, 0):
                pltpu.make_async_copy(src, t_all.at[mine, :], t_recv.at[z]).start()
            else:
                remote(
                    src, t_all.at[mine, :], t_send.at[index * n_grp + i], t_recv.at[z], (e, a * SIDE + y), sent
                )

    def sent(name, index):
        for copy in in_flight.pop((name, index)):
            copy.wait_send()

    step = 256

    def turn(i, carry):
        rows = pl.ds(pl.multiple_of(i * step, step), step)
        for j in range(height // step):
            w_t[rows, j * step : (j + 1) * step] = w_in[j * step : (j + 1) * step, rows].T
        return carry

    def turn_weight():
        load_w.wait()
        lax.fori_loop(0, breadth // step, turn, 0)

    def rows_of(zs, ys):
        return pl.ds(pl.multiple_of((zs * SIDE + ys) * chunk, chunk), chunk)

    def landed(ref, sem):
        pltpu.make_async_copy(ref, ref, sem).wait()

    def cut_of(kz):
        return (3 if kz in (0, 3) else 2) * step

    def cut_of(kz):
        return (3 if kz in (0, 3) else 2) * step

    def input_gradient(kz, k):
        cut = cut_of(kz)
        halves = {1: slice(cut, height), 2: slice(0, cut)}
        p = jnp.dot(g_all[rows_of(z_at(ORDER[kz]), y_at(ORDER[k])), :], w_t[...], preferred_element_type=F32)
        if k == 0:
            own_sum[kz] = p
            return
        slot = kz * 3 + k - 1
        src = rs_send.at[slot]
        if k == 3:
            rs_send[slot] = p.astype(BF16)
            for way, d in ((0, 3), (1, 1)):
                cols = halves[2 - way]
                sem = kz * 2 + way
                remote(
                    src.at[:, cols],
                    rs_half.at[kz, :, cols],
                    h_send.at[sem],
                    h_recv.at[sem],
                    (g, z * SIDE + y_at(d)),
                )
            return
        other = halves[3 - k]
        cols = halves[k]
        rs_send[slot, :, other] = p[:, other].astype(BF16)
        landed(rs_half.at[kz, :, cols], h_recv.at[kz * 2 + k % 2])
        rs_send[slot, :, cols] = (p[:, cols] + rs_half[kz, :, cols].astype(F32)).astype(BF16)
        slot = kz * 2 + k - 1
        remote(src, rs_recv.at[slot], r_send.at[slot], r_recv.at[slot], (g, z * SIDE + y_at(ORDER[k])))

    def reduce(kz):
        for slot in (kz * 2, kz * 2 + 1):
            landed(rs_recv.at[slot], r_recv.at[slot])
        half = 16

        def part(i, carry):
            rows = pl.ds(pl.multiple_of(i * half, half), half)
            lanes = lax.broadcasted_iota(jnp.int32, (half, QB), 1)
            scales = jnp.zeros((half, QB), F32)
            for j in range(height // QB):
                cols = slice(j * QB, (j + 1) * QB)
                total = own_sum[kz, rows, cols]
                for slot in (kz * 2, kz * 2 + 1):
                    total = total + rs_recv[slot, rows, cols].astype(F32)
                s = jnp.max(jnp.abs(total), axis=1, keepdims=True) + EPS
                back_send[kz, rows, cols] = (total * (1.0 / s)).astype(BF16)
                scales = jnp.where(lanes == j, s, scales)
            back_send[kz, rows, height:] = scales.astype(BF16)
            return carry

        lax.fori_loop(0, chunk // half, part, 0)
        zs = z_at(ORDER[kz])
        dst = back.at[pl.ds(pl.multiple_of((g * SIDE + z) * shard, shard), shard), :]
        for i, (dx, dc) in enumerate(x_order):
            r = grp_at(dx, dc)
            src = back_send.at[kz, pl.ds(pl.multiple_of(r * shard, shard), shard), :]
            if (dx, dc, kz) == (0, 0, 0):
                pltpu.make_async_copy(src, dst, b_recv).start()
            else:
                remote(src, dst, b_send.at[kz * n_grp + i], b_recv, (r, zs * SIDE + y))

    wide = 512

    def turn_tokens(kz):
        for u in range(block // step):
            rows = pl.ds(pl.multiple_of(z_at(ORDER[kz]) * block + u * step, step), step)

            def turn(i, carry):
                down = pl.ds(pl.multiple_of(i * step, step), step)
                w_in[down, rows] = t_all[rows, down].T
                return carry

            lax.fori_loop(0, height // step, turn, 0)

    def weight_gradient(kz, first, last):
        rows = pl.ds(pl.multiple_of(z_at(ORDER[kz]) * block, block), block)

        def col_step(j, carry):
            along = pl.ds(pl.multiple_of(j * wide, wide), wide)
            p = jnp.dot(w_in[:, rows], g_all[rows, along], preferred_element_type=F32)
            if not first:
                p = p + dw_sum[:, along]
            if not last:
                dw_sum[:, along] = p
                return carry
            at_row = lax.broadcasted_iota(jnp.int32, dw_scale.shape, 0)
            at_col = lax.broadcasted_iota(jnp.int32, dw_scale.shape, 1)
            scales = dw_scale[...]
            for u in range(height // QB):
                for v in range(wide // QB):
                    q = p[u * QB : (u + 1) * QB, v * QB : (v + 1) * QB]
                    s = jnp.max(jnp.max(jnp.abs(q), axis=0, keepdims=True), axis=1, keepdims=True) + EPS
                    cols = pl.ds(pl.multiple_of(j * wide + v * QB, QB), QB)
                    dw_quant[u * QB : (u + 1) * QB, cols] = (q * (1.0 / s)).astype(BF16)
                    scales = jnp.where((at_row == u) & (at_col == j * (wide // QB) + v), s, scales)
            dw_scale[...] = scales
            pltpu.make_async_copy(dw_quant.at[:, along], dw_out.at[:, along], out_sem.at[j]).start()
            return carry

        lax.fori_loop(0, breadth // wide, col_step, 0)

    def half_of(zs, ys, upper):
        start = (zs * SIDE + ys) * chunk + (chunk // 2 if upper else 0)
        return pl.ds(pl.multiple_of(start, chunk // 2), chunk // 2)

    def pass_on(buffer, rows, send, recv, device):
        remote(buffer.at[rows, :], buffer.at[rows, :], send, recv, device)

    def grad_own(k):
        rows = rows_of(z, y_at(ORDER[k]))
        landed(g_all.at[rows, :], g_recv.at[y_at(ORDER[k])])
        for way, d in enumerate((1, 3)):
            sem = way * SIDE + k
            pass_on(g_all, rows, z_send.at[sem], z_recv.at[sem], (g, z_at(d) * SIDE + y))

    def grad_near(k):
        for way, d in enumerate((1, 3)):
            landed(g_all.at[rows_of(z_at(-d), y_at(ORDER[k])), :], z_recv.at[way * SIDE + k])

    def grad_on(k):
        for way, d in enumerate((1, 3)):
            rows = half_of(z_at(-d), y_at(ORDER[k]), way == 0)
            sem = (2 + way) * SIDE + k
            pass_on(g_all, rows, z_send.at[sem], z_recv.at[sem], (g, z_at(d) * SIDE + y))

    def grad_far(k):
        for way in range(2):
            rows = half_of(z_at(2), y_at(ORDER[k]), way == 0)
            landed(g_all.at[rows, :], z_recv.at[(2 + way) * SIDE + k])

    def tokens_own(k):
        rows = rows_of(z_at(ORDER[k]), y)
        landed(t_all.at[rows, :], t_recv.at[z_at(ORDER[k])])
        for way, d in enumerate((1, 3)):
            sem = way * SIDE + k
            pass_on(t_all, rows, y_send.at[sem], y_recv.at[sem], (g, z * SIDE + y_at(d)))

    def tokens_near(k):
        for way, d in enumerate((1, 3)):
            landed(t_all.at[rows_of(z_at(ORDER[k]), y_at(-d)), :], y_recv.at[way * SIDE + k])
            rows = half_of(z_at(ORDER[k]), y_at(-d), way == 0)
            sem = (2 + way) * SIDE + k
            pass_on(t_all, rows, y_send.at[sem], y_recv.at[sem], (g, z * SIDE + y_at(d)))

    def tokens_far(k):
        for way in range(2):
            rows = half_of(z_at(ORDER[k]), y_at(2), way == 0)
            landed(t_all.at[rows, :], y_recv.at[(2 + way) * SIDE + k])

    dw_scale[...] = jnp.zeros(dw_scale.shape, F32)
    actions = {
        "grad": send_grad,
        "tokens": send_tokens,
        "grad_sent": functools.partial(sent, "grad"),
        "tokens_sent": functools.partial(sent, "tokens"),
        "turn": turn_weight,
        "grad_own": grad_own,
        "grad_near": grad_near,
        "grad_on": grad_on,
        "turn_tokens": turn_tokens,
        "grad_far": grad_far,
        "tokens_own": tokens_own,
        "tokens_near": tokens_near,
        "tokens_far": tokens_far,
        "dx": input_gradient,
        "reduce": reduce,
        "dw": weight_gradient,
    }
    for name, *numbers in STEPS:
        actions[name](*numbers)

    for j in range(breadth // wide):
        along = pl.ds(j * wide, wide)
        pltpu.make_async_copy(dw_quant.at[:, along], dw_out.at[:, along], out_sem.at[j]).wait()
    for copy in sum(in_flight.values(), waits):
        copy.wait_send()
    landed(back, b_recv)


def on_device(dy_quant, dy_scale, tokens, weight, counts):
    n_grp, _, shard, hidden = dy_quant.shape
    width = tokens.shape[-1]
    height, breadth = weight.shape[-2:]
    rows = n_grp * shard
    slots = SIDE * SIDE * rows
    dma = pltpu.SemaphoreType.DMA
    back, dw_quant, dw_scale = pl.pallas_call(
        functools.partial(kernel, (n_grp, shard, height, breadth)),
        out_shape=(
            jax.ShapeDtypeStruct((n_grp * SIDE * shard, height + QB), BF16),
            jax.ShapeDtypeStruct((height, breadth), BF16),
            jax.ShapeDtypeStruct((height // QB, breadth // QB), F32),
        ),
        in_specs=[
            pl.BlockSpec(memory_space=pltpu.SMEM),
            pl.BlockSpec(memory_space=pltpu.VMEM),
            pl.BlockSpec(memory_space=pl.ANY),
            pl.BlockSpec(memory_space=pl.ANY),
            pl.BlockSpec(memory_space=pl.ANY),
        ],
        out_specs=(
            pl.BlockSpec(memory_space=pl.ANY),
            pl.BlockSpec(memory_space=pl.ANY),
            pl.BlockSpec(memory_space=pltpu.VMEM),
        ),
        scratch_shapes=[
            pltpu.VMEM((rows, hidden), BF16),
            pltpu.VMEM((rows, hidden), BF16),
            pltpu.VMEM((height, breadth), BF16),
            pltpu.VMEM((breadth, height), BF16),
            pltpu.VMEM((slots, breadth), BF16),
            pltpu.VMEM((slots, height), BF16),
            pltpu.VMEM((12, rows, height), BF16),
            pltpu.VMEM((SIDE, rows, height), BF16),
            pltpu.VMEM((8, rows, height), BF16),
            pltpu.VMEM((SIDE, rows, height), F32),
            pltpu.VMEM((SIDE, rows, height + QB), BF16),
            pltpu.VMEM((height, breadth), F32),
            pltpu.VMEM((height, breadth), BF16),
            dma((2,)),
            dma((SIDE * n_grp,)),
            dma((SIDE,)),
            dma((SIDE * n_grp,)),
            dma((SIDE,)),
            dma((16,)),
            dma((16,)),
            dma((16,)),
            dma((16,)),
            dma((8,)),
            dma((8,)),
            dma((8,)),
            dma((8,)),
            dma((SIDE * n_grp,)),
            dma,
            dma((breadth // 512,)),
        ],
        compiler_params=pltpu.CompilerParams(
            collective_id=0, has_side_effects=True, vmem_limit_bytes=62 * 2**20
        ),
        name="up_backward",
    )(
        counts,
        dy_scale.reshape(rows, hidden // QB),
        dy_quant.reshape(rows, hidden),
        tokens.reshape(rows, width),
        weight.reshape(height, breadth),
    )
    dx_quant, dx_scale, dw_quant = finish(
        back.reshape(n_grp, SIDE, shard, height + QB), dw_quant
    )
    return (dx_quant[:, None], dx_scale[:, None], dw_quant[None, None], dw_scale[None, None])


def finish_kernel(back, dw, dx_out, scale_out, dw_out, scales, dx, dw_in, scale_sem, dx_sem, dw_sem):
    n_grp, parts, shard, width = back.shape
    height = width - QB
    groups = height // QB
    loads = []
    for a in range(parts):
        cols = slice(a * height, (a + 1) * height)
        loads.append(pltpu.make_async_copy(back.at[:, a, :, :height], dx.at[:, :, cols], dx_sem.at[0, a]))
    piece = dw.shape[0] // dw_sem.shape[1]
    for i in range(dw_sem.shape[1]):
        rows = slice(i * piece, (i + 1) * piece)
        loads.append(pltpu.make_async_copy(dw.at[rows], dw_in.at[rows], dw_sem.at[0, i]))
    load = pltpu.make_async_copy(back.at[:, :, :, height:], scales, scale_sem)
    for copy in loads:
        copy.start()
    load.start()
    copies = []
    for a in range(parts):
        loads[a].wait()
    for a in range(2):
        part = slice(a * n_grp // 2, (a + 1) * n_grp // 2)
        copies.append(pltpu.make_async_copy(dx.at[part], dx_out.at[part], dx_sem.at[1, a]))
        copies[-1].start()
    for i in range(dw_sem.shape[1]):
        loads[parts + i].wait()
        rows = slice(i * piece, (i + 1) * piece)
        copies.append(pltpu.make_async_copy(dw_in.at[rows], dw_out.at[rows], dw_sem.at[1, i]))
        copies[-1].start()
    load.wait()
    for e in range(n_grp):
        line = [scales[e, a][:, :groups] for a in range(parts)]
        scale_out[e] = jnp.concatenate(line, axis=1)
    for copy in copies:
        copy.wait()


def finish(back, dw):
    n_grp, parts, shard, width = back.shape
    height = width - QB
    anywhere = pl.BlockSpec(memory_space=pl.ANY)
    dma = pltpu.SemaphoreType.DMA
    return pl.pallas_call(
        finish_kernel,
        out_shape=(
            jax.ShapeDtypeStruct((n_grp, shard, parts * height), BF16),
            jax.ShapeDtypeStruct((n_grp, shard, parts * height // QB), BF16),
            jax.ShapeDtypeStruct(dw.shape, BF16),
        ),
        in_specs=[anywhere, anywhere],
        out_specs=(anywhere, pl.BlockSpec(memory_space=pltpu.VMEM), anywhere),
        scratch_shapes=[
            pltpu.VMEM((n_grp, parts, shard, QB), BF16),
            pltpu.VMEM((n_grp, shard, parts * height), BF16),
            pltpu.VMEM(dw.shape, BF16),
            dma,
            dma((2, parts)),
            dma((2, 5)),
        ],
        compiler_params=pltpu.CompilerParams(vmem_limit_bytes=62 * 2**20),
        name="finish",
    )(back, dw)


def solution(mesh):
    return jax.shard_map(
        on_device,
        mesh=mesh,
        in_specs=(
            P(None, "grp", "grid", None),
            P(None, "grp", "grid", None),
            P(None, "grp", "grid", None),
            P("grp", "grid", None, None),
            P(),
        ),
        out_specs=(
            P(None, "grp", "grid", None),
            P(None, "grp", "grid", None),
            P("grp", "grid", None, None),
            P("grp", "grid", None, None),
        ),
        check_vma=False,
    )
```
